256 devices in a mesh: ctx: 32 (over z_lo, y, core), exp: 8 (over z_hi, x).
Axes of the slice: x: 4, y: 4, z: 8 (z_hi: 2, z_lo: 4; z = z_hi * 4 + z_lo), core: 2. Of those that a mesh axis runs over, the one named last changes fastest.
Arguments:
- hidden_in: bfloat16 [32768, 2048], P(('ctx', 'exp')), may hold values from -6 to 6
- queries: bfloat16 [32768, 2048], P(('ctx', 'exp')), may hold values from -140 to 140
- keys: bfloat16 [32768, 256], P(('ctx', 'exp')), may hold values from -4.5 to 4.5
- values: bfloat16 [32768, 256], P(('ctx', 'exp')), may hold values from -6 to 6
- doc_ids: int32 [32768], P(('ctx', 'exp')), may hold values from 0 to 255, never falling along the last dimension, each value on 1 to 256 neighbouring positions
- norm_gain: float32 [2048], replicated, may hold values from 0.5 to 1.5
- expert_ids: int32 [32768, 4], P(('ctx', 'exp')), may hold values from 0 to 127, all different within a row; in each aligned block of 128 rows (0 to 127, 128 to 255, ...) at most 6 rows name the same one
- gate_weights: float32 [32768, 4], P(('ctx', 'exp')), may hold values from 0.1 to 1
- w_gate_up: bfloat16 [256, 2048, 384], P(('ctx', 'exp')), may hold values from -0.125 to 0.125
- w_down: bfloat16 [256, 192, 2048], P(('ctx', 'exp')), may hold values from -0.3125 to 0.3125
- grad_out: bfloat16 [32768, 2048], P(('ctx', 'exp')), may hold values from -6 to 6
Outputs:
- output: bfloat16 [32768, 2048], P(('ctx', 'exp'))
- grad_in: bfloat16 [32768, 2048], P(('ctx', 'exp'))
- grad_queries: bfloat16 [32768, 2048], P(('ctx', 'exp'))
- grad_keys: float32 [32768, 256], P(('ctx', 'exp'))
- grad_values: float32 [32768, 256], P(('ctx', 'exp'))
- grad_gate_up: float32 [256, 2048, 384], P(('ctx', 'exp'))
- grad_down: float32 [256, 192, 2048], P(('ctx', 'exp'))
The draws below stay inside these ranges and needn't reach their ends.
Inputs may be any that keep to these rules, and one draw needn't show every extreme that they name: `doc_ids`: document numbers never fall along the sequence, and one document holds at most 256 positions. `expert_ids`: A row names 4 different experts. Among the rows of one device no expert is named more than 6 times.
All inputs are finite; a program needn't handle non-finite values.
Results may differ from the reference program's by a relative error of at most 0.023.
Values may be sent and summed in bfloat16 or wider, within the bound.
No kernel may reach another device: no remote copies, remote signals or barrier semaphores. Data moves between devices by JAX's collectives and lax.ppermute only.
A program may use at most 192 MiB of HBM per device.

```python
import math
import jax
import jax.numpy as jnp
import numpy as np
from jax import lax

D = 2048
HEADS = 16
KV_HEADS = 2
HEAD_DIM = 128
GROUP = 8
FF = 384
HALF = 192
TOP = 4
RIM = 2
TOK_DEV = 128
SEQ = 32768
EXPERTS = 128
CAP = 6
DOCS = 256
DEVICES = 256


def shared_keys(key):
    return jax.random.truncated_normal(jax.random.fold_in(key, 7), -4.5, 4.5, (SEQ, KV_HEADS * HEAD_DIM), jnp.float32)


def draw_keys(key, part):
    base_keys = shared_keys(key)
    return base_keys.astype(jnp.bfloat16)


def draw_queries(key, part):
    key = jax.random.fold_in(key, 2)
    drawn_draw = jax.random.truncated_normal(key, -4.5, 4.5, (SEQ, HEADS * HEAD_DIM), jnp.float32)
    return drawn_draw.astype(jnp.bfloat16)


def levels(own_key, extent, shards, low, high):
    gain, own = 1.0, jax.random.fold_in(own_key, 6)
    for position, shards_of in shards:
        heights = jnp.exp(jax.random.uniform(jax.random.fold_in(own, position), (shards_of,), jnp.float32, low / len(shards), high / len(shards)))
        gain = gain * jnp.repeat(heights, extent[position] // shards_of).reshape([-1 if axis == position else 1 for axis in range(len(extent))])
    return gain


def split_up(number_of, total, most, skew):
    portions = [(1 << 20) // math.isqrt(rank ** skew) + 1 for rank in range(2, number_of + 1)]
    surplus, given = total - most - (number_of - 1), [1] * (number_of - 1)
    while surplus > 0:
        movable = [i for i in range(number_of - 1) if given[i] < most]
        pool, remaining = sum([portions[i] for i in movable]), surplus
        for i in movable:
            extra = min(most - given[i], max(1, remaining * portions[i] // pool), surplus)
            given[i] = given[i] + extra
            surplus = surplus - extra
    return np.array([most] + given)


def uneven(own_key, amount, total, limit, lean):
    if amount == 2:
        one = jax.random.randint(own_key, (), max(1, total - limit), min(limit, total - 1) + 1)
        return jnp.stack([one, total - one])
    tallies = jnp.asarray(split_up(amount, total, limit, lean), jnp.int32)
    pairs = (amount - 1) // 2
    donor, sink = tallies[1:1 + 2 * pairs:2], tallies[2:2 + 2 * pairs:2]
    margin = jnp.minimum(donor - 1, limit - sink)
    passed = jax.random.randint(jax.random.fold_in(own_key, 1), (pairs,), 0, 1 << 20) % (margin + 1)
    tallies = tallies.at[1:1 + 2 * pairs:2].set(donor - passed).at[2:2 + 2 * pairs:2].set(sink + passed)
    return tallies[jax.random.permutation(jax.random.fold_in(own_key, 2), amount)]


def assign_block(key, own, number, rows, count, top, bound, skew):
    sequence = jax.random.permutation(key, count)
    heavy_load, common = portions_of(count, rows * top, bound, skew, True), portions_of(count, rows * top, bound, skew, False)
    places = jnp.arange(count)

    def named(tallies, turn):
        used = int((tallies > 0).sum())
        fixed = max(1, used // 4)
        moved = fixed + (places - fixed + turn * (used - fixed)) % max(1, count - fixed)
        return jnp.zeros((count,), jnp.int32).at[sequence[jnp.where(places < fixed, places, moved)]].set(jnp.asarray(tallies, jnp.int32))

    tallies = jnp.where(number % 4 == 0, named(heavy_load, number // 4), named(common, number - number // 4 - 1))
    mixed = jax.random.permutation(jax.random.fold_in(own, 3), count)
    source_of, receiver = mixed[0:count // 2 * 2:2], mixed[1:count // 2 * 2:2]
    slack = jnp.minimum(tallies[source_of] - 1, bound - tallies[receiver]) // 2
    slack = jnp.where((source_of == sequence[0]) | (receiver == sequence[0]) | (tallies[receiver] == 0), 0, jnp.maximum(slack, 0))
    moved = jax.random.randint(jax.random.fold_in(own, 4), (count // 2,), 0, 1 << 20) % (slack + 1)
    tallies = tallies.at[source_of].add(-moved).at[receiver].add(moved)
    items = jnp.searchsorted(jnp.cumsum(tallies), jnp.arange(rows * top), side="right").astype(jnp.int32)
    grid = items.reshape(top, rows).T
    grid = grid[jax.random.permutation(jax.random.fold_in(own, 1), rows)]
    turn = jax.random.randint(jax.random.fold_in(own, 2), (rows, 1), 0, top)
    return jnp.take_along_axis(grid, (jnp.arange(top)[None, :] + turn) % top, axis=1)


def portions_of(number_of, total, limit, skew, full):
    portions = [(1 << 20) // math.isqrt(grade ** skew) + 1 for grade in range(1, number_of + 1)]
    largest = limit if full else min(limit, max(-(-total // number_of), total * portions[0] // sum(portions)))
    least = 1 if total - largest >= number_of - 1 else 0
    holding, surplus = [largest] + [least] * (number_of - 1), total - largest - least * (number_of - 1)
    while surplus > 0:
        free = [i for i in range(1, number_of) if holding[i] < largest] or [i for i in range(1, number_of) if holding[i] < limit]
        whole, left = sum([portions[i] for i in free]), surplus
        for i in free:
            extra = min(limit - holding[i], max(1, left * portions[i] // whole), surplus)
            holding[i] = holding[i] + extra
            surplus = surplus - extra
    return np.array(holding)


def bell_draw(key, dims, width, most, cuts=(), held_as=jnp.bfloat16):
    gain = levels(key, dims, cuts, -0.22, 0.18) if cuts else 1.0
    values = jax.random.normal(key, dims, jnp.float32) * width * gain
    return jnp.minimum(jnp.maximum(values, -most), most).astype(held_as)


def setup_inputs(seed: int = 0) -> dict:
    arg_keys = jax.random.split(jax.random.key(seed), 12)
    hidden_in = bell_draw(arg_keys[0], (SEQ, D), 1.0, 6.0, ((0, 256),))
    queries = draw_queries(jax.random.fold_in(arg_keys[11], 71), 0)
    keys = draw_keys(jax.random.fold_in(arg_keys[11], 71), 0)
    values = bell_draw(arg_keys[3], (SEQ, KV_HEADS * HEAD_DIM), 1.0, 6.0, ((0, 256),))
    doc_ids = jnp.searchsorted(jnp.cumsum(uneven(arg_keys[4], DOCS, SEQ, RIM * TOK_DEV, 2)), jnp.arange(SEQ), side="right").astype(jnp.int32)
    norm_gain = jnp.clip(1.0 + 0.1 * jax.random.normal(arg_keys[5], (D,), jnp.float32), 0.5, 1.5)
    expert_ids_keys = jax.random.split(jax.random.fold_in(arg_keys[6], 1), SEQ // TOK_DEV)
    expert_ids_turns = jax.random.permutation(jax.random.fold_in(arg_keys[6], 3), SEQ // TOK_DEV)
    expert_ids = jax.vmap(lambda own, number: assign_block(jax.random.fold_in(arg_keys[6], 2), own, number, TOK_DEV, EXPERTS, TOP, CAP, 2))(expert_ids_keys, expert_ids_turns).reshape((SEQ, TOP))
    gate_weights = jnp.clip(0.1 + 0.9 * jax.random.uniform(arg_keys[7], (SEQ, TOP), jnp.float32) ** levels(arg_keys[7], (SEQ, TOP), ((0, 256),), -0.2, 0.2), 0.1, 1.0)
    w_gate_up = bell_draw(arg_keys[8], (2 * EXPERTS, D, FF), D ** -0.5, 0.125, ((0, 256),))
    w_down = bell_draw(arg_keys[9], (2 * EXPERTS, HALF, D), FF ** -0.5, 0.3125, ((0, 256),))
    grad_out = bell_draw(arg_keys[10], (SEQ, D), 1.0, 6.0, ((0, 256),))
    return {"hidden_in": hidden_in, "queries": queries, "keys": keys, "values": values, "doc_ids": doc_ids, "norm_gain": norm_gain, "expert_ids": expert_ids, "gate_weights": gate_weights, "w_gate_up": w_gate_up, "w_down": w_down, "grad_out": grad_out}


EPSILON = 1e-06
MASKED = -1e+30

def attend_window(query_rows, window_keys, window_values, visible):
    scale_factor = HEAD_DIM ** (-0.5)
    row_count = query_rows.shape[0]
    query_heads = query_rows.astype(jnp.float32).reshape(row_count, KV_HEADS, GROUP, HEAD_DIM)
    key_heads = window_keys.astype(jnp.float32).reshape(-1, KV_HEADS, HEAD_DIM)
    value_heads = window_values.astype(jnp.float32).reshape(-1, KV_HEADS, HEAD_DIM)
    scores = jnp.einsum('qgmd,kgd->gmqk', query_heads, key_heads) * scale_factor
    scores = jnp.where(visible[None, None], scores, MASKED)
    row_max = lax.optimization_barrier(jnp.max(scores, axis=3, keepdims=True))
    exp_terms = jnp.exp(scores - row_max)
    attn_probs = exp_terms / lax.optimization_barrier(jnp.sum(exp_terms, axis=3, keepdims=True))
    probs_low = attn_probs.astype(jnp.bfloat16)
    mixed_heads = jnp.einsum('gmqk,kgd->qgmd', probs_low.astype(jnp.float32), value_heads)
    return (mixed_heads.reshape(row_count, HEADS * HEAD_DIM).astype(jnp.bfloat16), attn_probs, probs_low)

def attend_grad(query_rows, window_keys, window_values, attn_out, grad_rows, attn_probs, probs_low):
    scale_factor = HEAD_DIM ** (-0.5)
    row_count = query_rows.shape[0]
    query_heads = query_rows.astype(jnp.float32).reshape(row_count, KV_HEADS, GROUP, HEAD_DIM)
    key_heads = window_keys.astype(jnp.float32).reshape(-1, KV_HEADS, HEAD_DIM)
    value_heads = window_values.astype(jnp.float32).reshape(-1, KV_HEADS, HEAD_DIM)
    grad_heads = grad_rows.astype(jnp.float32).reshape(row_count, KV_HEADS, GROUP, HEAD_DIM)
    out_heads = attn_out.astype(jnp.float32).reshape(row_count, KV_HEADS, GROUP, HEAD_DIM)
    row_dot = jnp.einsum('qgmd,qgmd->gmq', grad_heads, out_heads)
    grad_probs = jnp.einsum('qgmd,kgd->gmqk', grad_heads, value_heads)
    grad_scores = (attn_probs * (grad_probs - row_dot[..., None])).astype(jnp.bfloat16).astype(jnp.float32)
    grad_query = jnp.einsum('gmqk,kgd->qgmd', grad_scores, key_heads) * scale_factor
    grad_key = jnp.einsum('gmqk,qgmd->kgd', grad_scores, query_heads) * scale_factor
    grad_value = jnp.einsum('gmqk,qgmd->kgd', probs_low.astype(jnp.float32), grad_heads)
    return (grad_query.reshape(row_count, HEADS * HEAD_DIM).astype(jnp.bfloat16), grad_key.reshape(-1, KV_HEADS * HEAD_DIM), grad_value.reshape(-1, KV_HEADS * HEAD_DIM))

def expert_forward(in_rows, weight_in, weight_out):
    projected = jnp.dot(in_rows, weight_in, preferred_element_type=jnp.float32)
    gate_pre = projected[:, :HALF]
    up_pre = projected[:, HALF:]
    activated = (gate_pre * jax.nn.sigmoid(gate_pre) * up_pre).astype(jnp.bfloat16)
    half_out = jnp.dot(activated, weight_out, preferred_element_type=jnp.float32).astype(jnp.bfloat16)
    return (half_out, gate_pre, up_pre, activated)

def expert_backward(in_rows, grad_rows, weight_in, weight_out, gate_pre, up_pre, activated):
    grad_act = jnp.dot(grad_rows, weight_out.T, preferred_element_type=jnp.float32)
    grad_weight_out = jnp.dot(activated.T, grad_rows, preferred_element_type=jnp.float32)
    sigmoid_gate = jax.nn.sigmoid(gate_pre)
    grad_gate = grad_act * up_pre * sigmoid_gate * (1.0 + gate_pre * (1.0 - sigmoid_gate))
    grad_up = grad_act * gate_pre * sigmoid_gate
    grad_pre = jnp.concatenate([grad_gate, grad_up], axis=1).astype(jnp.bfloat16)
    grad_weight_in = jnp.dot(in_rows.T, grad_pre, preferred_element_type=jnp.float32)
    grad_half = jnp.dot(grad_pre, weight_in.T, preferred_element_type=jnp.float32).astype(jnp.bfloat16)
    return (grad_half, grad_weight_in, grad_weight_out)

def reference(hidden_in, queries, keys, values, doc_ids, norm_gain, expert_ids, gate_weights, w_gate_up, w_down, grad_out):
    window_len = (RIM + 1) * TOK_DEV
    front_rows = RIM * TOK_DEV
    keys_pad = jnp.concatenate([jnp.zeros((front_rows, keys.shape[1]), keys.dtype), keys], axis=0)
    values_pad = jnp.concatenate([jnp.zeros((front_rows, values.shape[1]), values.dtype), values], axis=0)
    docs_pad = jnp.concatenate([jnp.full((front_rows,), -1, jnp.int32), doc_ids.astype(jnp.int32)], axis=0)
    local_rows = jnp.arange(TOK_DEV, dtype=jnp.int32)
    window_rows = jnp.arange(window_len, dtype=jnp.int32)

    def piece_inputs(piece_index):
        start_row = (piece_index * TOK_DEV).astype(jnp.int32)
        query_rows = lax.dynamic_slice_in_dim(queries, start_row, TOK_DEV, 0)
        window_keys = lax.dynamic_slice_in_dim(keys_pad, start_row, window_len, 0)
        window_values = lax.dynamic_slice_in_dim(values_pad, start_row, window_len, 0)
        query_docs = lax.dynamic_slice_in_dim(doc_ids, start_row, TOK_DEV, 0)
        key_docs = lax.dynamic_slice_in_dim(docs_pad, start_row, window_len, 0)
        query_pos = start_row + local_rows
        key_pos = start_row - front_rows + window_rows
        visible = (query_docs[:, None] == key_docs[None, :]) & (key_pos[None, :] <= query_pos[:, None]) & (key_pos[None, :] >= 0)
        return (query_rows, window_keys, window_values, visible)

    def forward_piece(piece_index):
        query_rows, window_keys, window_values, visible = piece_inputs(piece_index)
        return attend_window(query_rows, window_keys, window_values, visible)[0]
    pieces = jnp.arange(DEVICES, dtype=jnp.int32)
    attn_out = lax.map(forward_piece, pieces).reshape(SEQ, HEADS * HEAD_DIM)
    residual = hidden_in.astype(jnp.float32) + attn_out.astype(jnp.float32)
    inv_rms = lax.rsqrt(lax.optimization_barrier(jnp.mean(residual * residual, axis=1, keepdims=True)) + EPSILON)
    normed = (residual * inv_rms * norm_gain).astype(jnp.bfloat16)
    slot_total = DEVICES * CAP
    flat_ids = expert_ids.astype(jnp.int32).reshape(DEVICES, TOK_DEV * TOP)
    expert_range = jnp.arange(EXPERTS, dtype=jnp.int32)
    onehot = (flat_ids[:, :, None] == expert_range[None, None, :]).astype(jnp.int32)
    slot_rank = lax.optimization_barrier(jnp.sum((jnp.cumsum(onehot, axis=1) - 1) * onehot, axis=2))
    device_of = jnp.arange(DEVICES, dtype=jnp.int32)[:, None]
    slot_position = (flat_ids * slot_total + device_of * CAP + slot_rank).reshape(-1)
    token_of = (device_of * TOK_DEV + jnp.arange(TOK_DEV * TOP, dtype=jnp.int32)[None, :] // TOP).reshape(-1)
    slot_token = jnp.full((EXPERTS * slot_total,), SEQ, jnp.int32).at[slot_position].set(token_of)
    slot_gate = jnp.zeros((EXPERTS * slot_total,), jnp.float32).at[slot_position].set(gate_weights.reshape(-1))
    normed_pad = jnp.concatenate([normed, jnp.zeros((1, D), jnp.bfloat16)], axis=0)
    grad_pad = jnp.concatenate([grad_out, jnp.zeros((1, D), grad_out.dtype)], axis=0)

    def expert_step(carried, expert_index):
        moe_acc, back_acc = carried
        slot_rows = lax.dynamic_slice_in_dim(slot_token, expert_index * slot_total, slot_total, 0)
        slot_scale = lax.dynamic_slice_in_dim(slot_gate, expert_index * slot_total, slot_total, 0)
        in_rows = normed_pad[slot_rows]
        grad_rows = (slot_scale[:, None] * grad_pad[slot_rows].astype(jnp.float32)).astype(jnp.bfloat16)
        expert_sum = jnp.zeros((slot_total, D), jnp.float32)
        back_sum = jnp.zeros((slot_total, D), jnp.float32)
        gate_grads = []
        down_grads = []
        for half_index in range(2):
            weight_in = lax.dynamic_index_in_dim(w_gate_up, 2 * expert_index + half_index, 0, keepdims=False)
            weight_out = lax.dynamic_index_in_dim(w_down, 2 * expert_index + half_index, 0, keepdims=False)
            half_out, gate_pre, up_pre, activated = expert_forward(in_rows, weight_in, weight_out)
            grad_half, grad_weight_in, grad_weight_out = expert_backward(in_rows, grad_rows, weight_in, weight_out, gate_pre, up_pre, activated)
            expert_sum = expert_sum + half_out.astype(jnp.float32)
            back_sum = back_sum + grad_half.astype(jnp.float32)
            gate_grads.append(grad_weight_in)
            down_grads.append(grad_weight_out)
        expert_out = expert_sum.astype(jnp.bfloat16).astype(jnp.float32)
        expert_grad = back_sum.astype(jnp.bfloat16).astype(jnp.float32)
        moe_acc = moe_acc.at[slot_rows].add(slot_scale[:, None] * expert_out)
        back_acc = back_acc.at[slot_rows].add(expert_grad)
        return ((moe_acc, back_acc), (jnp.stack(gate_grads), jnp.stack(down_grads)))
    start_acc = (jnp.zeros((SEQ + 1, D), jnp.float32), jnp.zeros((SEQ + 1, D), jnp.float32))
    (moe_acc, back_acc), (gate_stack, down_stack) = lax.scan(expert_step, start_acc, expert_range)
    output = (residual + moe_acc[:SEQ]).astype(jnp.bfloat16)
    grad_gate_up = gate_stack.reshape(2 * EXPERTS, D, FF)
    grad_down = down_stack.reshape(2 * EXPERTS, HALF, D)
    scaled = norm_gain * back_acc[:SEQ]
    grad_resid = grad_out.astype(jnp.float32) + inv_rms * scaled - residual * inv_rms ** 3 * lax.optimization_barrier(jnp.mean(residual * scaled, axis=1, keepdims=True))
    grad_in = grad_resid.astype(jnp.bfloat16)

    def backward_piece(carried, piece_index):
        key_acc, value_acc = carried
        query_rows, window_keys, window_values, visible = piece_inputs(piece_index)
        piece_out, attn_probs, probs_low = attend_window(query_rows, window_keys, window_values, visible)
        start_row = (piece_index * TOK_DEV).astype(jnp.int32)
        grad_rows = lax.dynamic_slice_in_dim(grad_in, start_row, TOK_DEV, 0)
        grad_query, grad_key, grad_value = attend_grad(query_rows, window_keys, window_values, piece_out, grad_rows, attn_probs, probs_low)
        key_acc = lax.dynamic_update_slice_in_dim(key_acc, lax.dynamic_slice_in_dim(key_acc, start_row, window_len, 0) + grad_key, start_row, 0)
        value_acc = lax.dynamic_update_slice_in_dim(value_acc, lax.dynamic_slice_in_dim(value_acc, start_row, window_len, 0) + grad_value, start_row, 0)
        return ((key_acc, value_acc), grad_query)
    kv_width = KV_HEADS * HEAD_DIM
    start_grads = (jnp.zeros((front_rows + SEQ, kv_width), jnp.float32), jnp.zeros((front_rows + SEQ, kv_width), jnp.float32))
    (key_acc, value_acc), query_grads = lax.scan(backward_piece, start_grads, pieces)
    grad_queries = query_grads.reshape(SEQ, HEADS * HEAD_DIM)
    return (output, grad_in, grad_queries, key_acc[front_rows:], value_acc[front_rows:], grad_gate_up, grad_down)
```

```python
import jax
import jax.numpy as jnp
from jax import lax
from jax.experimental.layout import Layout, with_layout_constraint
from jax.sharding import Mesh
from jax.sharding import PartitionSpec as P

HEADS = 16
KV_HEADS = 2
HEAD_DIM = 128
GROUP = 8
HALF = 192
RIM = 2

PARTS_GRAD = 1
PARTS_ROWS = 1
PARTS_BACK = 1
PARTS_OUT = 1

EPSILON = 1e-06
MASKED = -1e30

ALL = ("zl", "y", "core", "zh", "x")
COLUMN = ("zh", "zl")
PLANE = ("y", "core", "x")

BF16 = jnp.bfloat16
F32 = jnp.float32


def passed_along(block, distance):
    count = lax.axis_size(ALL)
    route = [(i - distance, i) for i in range(count) if 0 <= i - distance < count]
    return lax.ppermute(block, ALL, route)


def attend_window(query_rows, window_keys, window_values, visible):
    scale_factor = HEAD_DIM ** (-0.5)
    row_count = query_rows.shape[0]
    query_heads = query_rows.reshape(row_count, KV_HEADS, GROUP, HEAD_DIM)
    key_heads = window_keys.reshape(-1, KV_HEADS, HEAD_DIM)
    value_heads = window_values.reshape(-1, KV_HEADS, HEAD_DIM)
    scores = (
        jnp.einsum("qgmd,kgd->gmqk", query_heads, key_heads, preferred_element_type=F32)
        * scale_factor
    )
    scores = jnp.where(visible[None, None], scores, MASKED)
    row_max = jnp.max(scores, axis=3, keepdims=True)
    exp_terms = jnp.exp(scores - row_max)
    attn_probs = exp_terms / jnp.sum(exp_terms, axis=3, keepdims=True)
    probs_low = attn_probs.astype(BF16)
    mixed_heads = jnp.einsum("gmqk,kgd->qgmd", probs_low, value_heads, preferred_element_type=F32)
    return (
        mixed_heads.reshape(row_count, HEADS * HEAD_DIM).astype(BF16),
        attn_probs,
        probs_low,
    )


def attend_grad(query_rows, window_keys, window_values, attn_out, grad_rows, attn_probs, probs_low):
    scale_factor = HEAD_DIM ** (-0.5)
    row_count = query_rows.shape[0]
    query_heads = query_rows.reshape(row_count, KV_HEADS, GROUP, HEAD_DIM)
    key_heads = window_keys.reshape(-1, KV_HEADS, HEAD_DIM)
    value_heads = window_values.reshape(-1, KV_HEADS, HEAD_DIM)
    grad_heads = grad_rows.reshape(row_count, KV_HEADS, GROUP, HEAD_DIM)
    out_heads = attn_out.reshape(row_count, KV_HEADS, GROUP, HEAD_DIM)
    row_dot = jnp.einsum("qgmd,qgmd->gmq", grad_heads.astype(F32), out_heads.astype(F32))
    grad_probs = jnp.einsum("qgmd,kgd->gmqk", grad_heads, value_heads, preferred_element_type=F32)
    grad_scores = (attn_probs * (grad_probs - row_dot[..., None])).astype(BF16)
    grad_query = (
        jnp.einsum("gmqk,kgd->qgmd", grad_scores, key_heads, preferred_element_type=F32)
        * scale_factor
    )
    grad_key = (
        jnp.einsum("gmqk,qgmd->kgd", grad_scores, query_heads, preferred_element_type=F32)
        * scale_factor
    )
    grad_value = jnp.einsum("gmqk,qgmd->kgd", probs_low, grad_heads, preferred_element_type=F32)
    return (
        grad_query.reshape(row_count, HEADS * HEAD_DIM).astype(BF16),
        grad_key.reshape(-1, KV_HEADS * HEAD_DIM),
        grad_value.reshape(-1, KV_HEADS * HEAD_DIM),
    )


def columns_of(array, parts):
    width = array.shape[1] // parts
    return [array[:, i * width : (i + 1) * width] for i in range(parts)]


def joined(parts):
    return parts[0] if len(parts) == 1 else jnp.concatenate(parts, axis=1)


def across_plane(rows):
    devices = lax.axis_size(PLANE)
    cut = rows.reshape(devices, rows.shape[0] // devices, rows.shape[1])
    return lax.all_to_all(cut, PLANE, 0, 0, tiled=True).reshape(rows.shape)


def routing_columns(expert_ids, gate_weights):
    high = lax.reduce_precision(gate_weights, 8, 7)
    middle = lax.reduce_precision(gate_weights - high, 8, 7)
    low = gate_weights - high - middle
    columns = jnp.concatenate([expert_ids.astype(F32), high, middle, low], axis=1).astype(BF16)
    return jnp.pad(columns, ((0, 0), (0, 128 - columns.shape[1])))


def route_slots(gathered, top):
    planes = lax.axis_size(COLUMN)
    per_plane = lax.axis_size(PLANE) // 2
    tokens = gathered.shape[0]
    depth = 3 * tokens * top // (2 * planes * per_plane)
    columns = gathered[:, : 4 * top].astype(F32).T
    ids = columns[:top].astype(jnp.int32)
    gates = columns[top : 2 * top] + columns[2 * top : 3 * top] + columns[3 * top :]
    place = jnp.arange(per_plane, dtype=jnp.int32)
    experts = (
        lax.axis_index("zl") * (per_plane * 2)
        + (place // 2) * 4
        + lax.axis_index("zh") * 2
        + place % 2
    )
    match = ids[:, None, :] == experts[None, :, None]
    named = jnp.any(match, axis=0)
    gate_of = jnp.sum(jnp.where(match, gates[:, None, :], 0.0), axis=0)
    token = jnp.arange(tokens, dtype=jnp.int32)
    before = (token[:, None] < token[None, :]).astype(BF16)
    rank = jnp.dot(named.astype(BF16), before, preferred_element_type=F32)
    rank = jnp.where(named, rank, -1.0).astype(jnp.int32)
    chosen = rank[:, None, :] == jnp.arange(depth, dtype=jnp.int32)[None, :, None]
    slot_gate = jnp.sum(jnp.where(chosen, gate_of[:, None, :], 0.0), axis=2).reshape(-1, 1)
    return chosen.astype(BF16).reshape(per_plane * depth, tokens), slot_gate


def shards(
    hidden_in,
    queries,
    keys,
    values,
    doc_ids,
    norm_gain,
    expert_ids,
    gate_weights,
    w_gate_up,
    w_down,
    grad_out,
):
    row_count = hidden_in.shape[0]
    device_index = lax.axis_index(ALL)
    kv_width = keys.shape[1]

    gathered = []

    def gather_column(part):
        if len(gathered) >= 2:
            part, gathered[-2] = lax.optimization_barrier((part, gathered[-2]))
        rows = lax.all_gather(part, COLUMN, axis=0, tiled=True)
        gathered.append(with_layout_constraint(rows, Layout((0, 1))))

    top = expert_ids.shape[1]
    pieces = columns_of(grad_out, PARTS_GRAD)
    first_width = pieces[0].shape[1]
    pieces[0] = jnp.concatenate([pieces[0], routing_columns(expert_ids, gate_weights)], axis=1)
    for piece in pieces:
        gather_column(piece)

    swap = [(i, i ^ 1) for i in range(lax.axis_size("x"))]
    own_in, own_down = w_gate_up[0], w_down[0]
    other_in = lax.ppermute(own_in, "x", swap)
    other_down = lax.ppermute(own_down, "x", swap)

    doc_columns = jnp.broadcast_to(doc_ids[:, None].astype(BF16), (row_count, HEAD_DIM))
    packed = jnp.concatenate([keys, values, doc_columns], axis=1)
    window = [passed_along(packed, d) for d in range(RIM, 0, -1)] + [packed]
    window_packed = jnp.concatenate(window, axis=0)
    window_keys = window_packed[:, :kv_width]
    window_values = window_packed[:, kv_width : 2 * kv_width]
    window_docs = window_packed[:, 2 * kv_width].astype(jnp.int32)
    query_pos = device_index * row_count + jnp.arange(row_count, dtype=jnp.int32)
    key_pos = (device_index - RIM) * row_count + jnp.arange((RIM + 1) * row_count, dtype=jnp.int32)
    visible = (
        (doc_ids[:, None] == window_docs[None, :])
        & (key_pos[None, :] <= query_pos[:, None])
        & (key_pos[None, :] >= 0)
    )
    attn_out, attn_probs, probs_low = attend_window(queries, window_keys, window_values, visible)
    residual = hidden_in.astype(F32) + attn_out.astype(F32)
    inv_rms = lax.rsqrt(jnp.mean(residual * residual, axis=1, keepdims=True) + EPSILON)
    normed = (residual * inv_rms * norm_gain).astype(BF16)
    normed, other_in, other_down = lax.optimization_barrier((normed, other_in, other_down))
    for piece in columns_of(normed, PARTS_ROWS):
        if PARTS_GRAD == 1:
            piece, gathered[0] = lax.optimization_barrier((piece, gathered[0]))
        gather_column(piece)
    grad_columns = gathered[:PARTS_GRAD]
    normed_columns = gathered[PARTS_GRAD:]
    chosen, slot_gate = route_slots(grad_columns[0][:, first_width:], top)
    grad_columns[0] = grad_columns[0][:, :first_width]

    weight_in = jnp.concatenate(
        [own_in[:, :HALF], other_in[:, :HALF], own_in[:, HALF:], other_in[:, HALF:]], axis=1
    )
    weight_out = jnp.concatenate([own_down, other_down], axis=0)
    grad_rows = joined(
        [
            across_plane(
                (jnp.dot(chosen, part, preferred_element_type=F32) * slot_gate).astype(BF16)
            )
            for part in grad_columns
        ]
    )
    grad_rows, normed_columns[0] = lax.optimization_barrier((grad_rows, normed_columns[0]))
    grad_act = lax.dot_general(
        grad_rows, weight_out, (((1,), (1,)), ((), ())), preferred_element_type=F32
    )
    in_rows = joined(
        [
            across_plane(jnp.dot(chosen, part, preferred_element_type=F32).astype(BF16))
            for part in normed_columns
        ]
    )
    projected = jnp.dot(in_rows, weight_in, preferred_element_type=F32)
    gate_pre = projected[:, : 2 * HALF]
    up_pre = projected[:, 2 * HALF :]
    sigmoid_gate = jax.nn.sigmoid(gate_pre)
    activated = (gate_pre * sigmoid_gate * up_pre).astype(BF16)
    grad_gate = (
        grad_act * up_pre * sigmoid_gate * (1.0 + gate_pre * (1.0 - sigmoid_gate))
    ).astype(BF16)
    grad_up = (grad_act * gate_pre * sigmoid_gate).astype(BF16)
    grad_pre = jnp.concatenate([grad_gate, grad_up], axis=1)

    def summed_over_plane(rows):
        partial = lax.dot_general(
            chosen, rows, (((0,), (0,)), ((), ())), preferred_element_type=F32
        ).astype(BF16)
        return lax.psum_scatter(partial, COLUMN, scatter_dimension=0, tiled=True)

    back_width = weight_in.shape[0] // PARTS_BACK
    back_parts = []
    for i in range(PARTS_BACK):
        rows = lax.dot_general(
            grad_pre,
            weight_in[i * back_width : (i + 1) * back_width],
            (((1,), (1,)), ((), ())),
            preferred_element_type=F32,
        ).astype(BF16)
        back_parts.append(across_plane(rows))
    def halves(both, first):
        return both[:, first * HALF : (first + 1) * HALF]

    def times_rows(left, right, out_type):
        return lax.dot_general(
            left, right, (((0,), (0,)), ((), ())), preferred_element_type=F32
        ).astype(out_type)

    own_pre = jnp.concatenate([halves(grad_gate, 0), halves(grad_up, 0)], axis=1)
    other_pre = jnp.concatenate([halves(grad_gate, 1), halves(grad_up, 1)], axis=1)
    sent_in = times_rows(in_rows, other_pre, BF16)
    sent_down = times_rows(halves(activated, 1), grad_rows, BF16)
    kept_in = times_rows(in_rows, own_pre, F32)
    kept_down = times_rows(halves(activated, 0), grad_rows, F32)
    out_rows = [
        jnp.dot(activated, part, preferred_element_type=F32).astype(BF16)
        for part in columns_of(weight_out, PARTS_OUT)
    ]
    back_parts[-1], out_rows[0], sent_in, sent_down, kept_in, kept_down = lax.optimization_barrier(
        (back_parts[-1], out_rows[0], sent_in, sent_down, kept_in, kept_down)
    )
    grad_normed = joined([summed_over_plane(part) for part in back_parts]).astype(F32)
    out_parts = [across_plane(part) for part in out_rows]
    out_parts[-1], sent_in, sent_down = lax.optimization_barrier(
        (out_parts[-1], sent_in, sent_down)
    )
    sent_in = lax.ppermute(sent_in, "x", swap)
    sent_down = lax.ppermute(sent_down, "x", swap)
    moe_out = joined(
        [summed_over_plane((part.astype(F32) * slot_gate).astype(BF16)) for part in out_parts]
    )

    scaled = norm_gain * grad_normed
    grad_resid = (
        grad_out.astype(F32)
        + inv_rms * scaled
        - residual * inv_rms**3 * jnp.mean(residual * scaled, axis=1, keepdims=True)
    )
    grad_in = grad_resid.astype(BF16)
    grad_queries, key_window_grad, value_window_grad = attend_grad(
        queries, window_keys, window_values, attn_out, grad_in, attn_probs, probs_low
    )
    window_grad = jnp.concatenate([key_window_grad, value_window_grad], axis=1)
    grad_queries, moe_out, sent_in, sent_down = lax.optimization_barrier(
        (grad_queries, moe_out, sent_in, sent_down)
    )
    output = (residual + moe_out.astype(F32)).astype(BF16)
    grad_weight_in = kept_in + sent_in.astype(F32)
    grad_weight_out = kept_down + sent_down.astype(F32)
    own_grad = window_grad[RIM * row_count :]
    for distance in range(1, RIM + 1):
        start_row = (RIM - distance) * row_count
        own_grad = own_grad + passed_along(
            window_grad[start_row : start_row + row_count].astype(BF16), -distance
        ).astype(F32)
    return (
        output,
        grad_in,
        grad_queries,
        own_grad[:, :kv_width],
        own_grad[:, kv_width:],
        grad_weight_in[None],
        grad_weight_out[None],
    )


def solution(mesh):
    named = Mesh(mesh.devices.reshape(4, 4, 2, 2, 4), ALL)
    rows = P(ALL, None)
    blocks = P(ALL, None, None)
    return jax.shard_map(
        shards,
        mesh=named,
        in_specs=(rows, rows, rows, rows, P(ALL), P(), rows, rows, blocks, blocks, rows),
        out_specs=(rows, rows, rows, rows, rows, blocks, blocks),
        check_vma=False,
    )
```

```python
import jax
import jax.numpy as jnp
from jax import lax
from jax.experimental import pallas as pl
from jax.experimental.layout import Layout, with_layout_constraint
from jax.experimental.pallas import tpu as pltpu
from jax.sharding import Mesh
from jax.sharding import PartitionSpec as P

HEADS = 16
KV_HEADS = 2
HEAD_DIM = 128
GROUP = 8
HALF = 192
RIM = 2

PARTS_GRAD = 1
PARTS_ROWS = 1
PARTS_BACK = 1
PARTS_OUT = 1

VMEM_LIMIT = 60 * 2**20

EPSILON = 1e-06
MASKED = -1e30

ALL = ("zl", "y", "core", "zh", "x")
COLUMN = ("zh", "zl")
PLANE = ("y", "core", "x")

BF16 = jnp.bfloat16
F32 = jnp.float32


def passed_along(block, distance, sources):
    count, line = lax.axis_size(ALL), lax.axis_size("x")
    route = [
        (i, i + distance) for i in range(count) if 0 <= i + distance < count and i % line in sources
    ]
    return lax.ppermute(block, ALL, route)


def blocks_before(block):
    place = lax.axis_index("x")
    near = passed_along(block, 1, (0, 1, 2, 3))
    direct = passed_along(block, 2, (1, 2))
    handed = passed_along(near, 1, (0, 1))
    return [jnp.where((place == 0) | (place == 3), direct, handed), near]


def sums_from_after(far, near):
    place = lax.axis_index("x")
    swap = [(i, i ^ 1) for i in range(lax.axis_size(ALL)) if i % lax.axis_size("x") < 2]
    swapped = lax.ppermute(far, ALL, swap)
    near = jnp.where(place == 0, (near.astype(F32) + swapped.astype(F32)).astype(BF16), near)
    from_near = passed_along(near, -1, (0, 1, 2, 3))
    from_far = passed_along(far, -2, (2, 3))
    from_swapped = passed_along(swapped, -3, (1,))
    return from_near.astype(F32) + jnp.where(place == 2, from_swapped, from_far).astype(F32)


def attend_window(query_rows, window_keys, window_values, visible):
    scale_factor = HEAD_DIM ** (-0.5)
    row_count = query_rows.shape[0]
    query_heads = query_rows.reshape(row_count, KV_HEADS, GROUP, HEAD_DIM)
    key_heads = window_keys.reshape(-1, KV_HEADS, HEAD_DIM)
    value_heads = window_values.reshape(-1, KV_HEADS, HEAD_DIM)
    scores = (
        jnp.einsum("qgmd,kgd->gmqk", query_heads, key_heads, preferred_element_type=F32)
        * scale_factor
    )
    scores = jnp.where(visible[None, None], scores, MASKED)
    row_max = jnp.max(scores, axis=3, keepdims=True)
    exp_terms = jnp.exp(scores - row_max)
    attn_probs = exp_terms / jnp.sum(exp_terms, axis=3, keepdims=True)
    probs_low = attn_probs.astype(BF16)
    mixed_heads = jnp.einsum("gmqk,kgd->qgmd", probs_low, value_heads, preferred_element_type=F32)
    return (
        mixed_heads.reshape(row_count, HEADS * HEAD_DIM).astype(BF16),
        attn_probs,
        probs_low,
    )


def attend_grad(query_rows, window_keys, window_values, attn_out, grad_rows, attn_probs, probs_low):
    scale_factor = HEAD_DIM ** (-0.5)
    row_count = query_rows.shape[0]
    query_heads = query_rows.reshape(row_count, KV_HEADS, GROUP, HEAD_DIM)
    key_heads = window_keys.reshape(-1, KV_HEADS, HEAD_DIM)
    value_heads = window_values.reshape(-1, KV_HEADS, HEAD_DIM)
    grad_heads = grad_rows.reshape(row_count, KV_HEADS, GROUP, HEAD_DIM)
    out_heads = attn_out.reshape(row_count, KV_HEADS, GROUP, HEAD_DIM)
    row_dot = jnp.einsum("qgmd,qgmd->gmq", grad_heads.astype(F32), out_heads.astype(F32))
    grad_probs = jnp.einsum("qgmd,kgd->gmqk", grad_heads, value_heads, preferred_element_type=F32)
    grad_scores = (attn_probs * (grad_probs - row_dot[..., None])).astype(BF16)
    grad_query = (
        jnp.einsum("gmqk,kgd->qgmd", grad_scores, key_heads, preferred_element_type=F32)
        * scale_factor
    )
    grad_key = (
        jnp.einsum("gmqk,qgmd->kgd", grad_scores, query_heads, preferred_element_type=F32)
        * scale_factor
    )
    grad_value = jnp.einsum("gmqk,qgmd->kgd", probs_low, grad_heads, preferred_element_type=F32)
    return (
        grad_query.reshape(row_count, HEADS * HEAD_DIM).astype(BF16),
        grad_key.reshape(-1, KV_HEADS * HEAD_DIM),
        grad_value.reshape(-1, KV_HEADS * HEAD_DIM),
    )


def columns_of(array, parts):
    width = array.shape[1] // parts
    return [array[:, i * width : (i + 1) * width] for i in range(parts)]


def joined(parts):
    return parts[0] if len(parts) == 1 else jnp.concatenate(parts, axis=1)


def across_plane(rows):
    pairs, line = lax.axis_size(PLANE) // lax.axis_size("x"), lax.axis_size("x")
    groups = [[i * line + x for i in range(pairs) for x in places] for places in ((0, 3), (1, 2))]
    count = len(groups[0])
    cut = rows.reshape(count, rows.shape[0] // count, rows.shape[1])
    moved = lax.all_to_all(cut, PLANE, 0, 0, axis_index_groups=groups, tiled=True)
    return moved.reshape(rows.shape)


def cost_of(flops, *arrays):
    return pl.CostEstimate(
        flops=flops,
        bytes_accessed=sum(x.size * x.dtype.itemsize for x in arrays),
        transcendentals=0,
    )


def pick_kernel(chosen_ref, rows_ref, *rest):
    out_ref = rest[-1]
    picked = jnp.dot(chosen_ref[...], rows_ref[...], preferred_element_type=F32)
    if len(rest) == 2:
        picked = picked * rest[0][...]
    out_ref[...] = picked.astype(out_ref.dtype)


def picked_rows(chosen, rows, width, scale=None):
    count, depth = chosen.shape
    tile = 512
    out = jax.ShapeDtypeStruct((count, width), BF16)
    whole = pl.BlockSpec((count, depth), lambda i: (0, 0), pipeline_mode=pl.Buffered(1))
    operands = [chosen, rows]
    specs = [whole, pl.BlockSpec((depth, tile), lambda i: (0, i))]
    if scale is not None:
        operands.append(scale)
        specs.append(pl.BlockSpec((count, 1), lambda i: (0, 0)))
    return pl.pallas_call(
        pick_kernel,
        grid=(width // tile,),
        out_shape=out,
        in_specs=specs,
        out_specs=pl.BlockSpec((count, tile), lambda i: (0, i)),
        compiler_params=pltpu.CompilerParams(vmem_limit_bytes=VMEM_LIMIT),
        cost_estimate=cost_of(2 * count * depth * width, chosen, rows, out),
    )(*operands)


def expert_kernel(rows_ref, weight_ref, grad_act_ref, half_ref, act_ref, gate_ref, up_ref):
    projected = jnp.dot(rows_ref[...], weight_ref[...], preferred_element_type=F32)
    gate_pre = projected[:, : 2 * HALF]
    up_pre = projected[:, 2 * HALF :]
    sigmoid_gate = jax.nn.sigmoid(gate_pre)
    silu = gate_pre * sigmoid_gate
    act_ref[...] = (silu * up_pre).astype(BF16)
    grad_act = grad_act_ref[...]
    grad_gate = (grad_act * up_pre * sigmoid_gate * (1.0 + gate_pre * (1.0 - sigmoid_gate))).astype(
        BF16
    )
    grad_up = (grad_act * silu).astype(BF16)
    gate_ref[...] = grad_gate
    up_ref[...] = grad_up
    half_ref[...] = lax.dot_general(
        jnp.concatenate([grad_gate, grad_up], axis=1),
        weight_ref[...],
        (((1,), (1,)), ((), ())),
        preferred_element_type=F32,
    ).astype(BF16)


def expert_rows(rows, weight_in, grad_act):
    count, width = rows.shape
    hidden = grad_act.shape[1]
    tile = 256
    by_rows = lambda columns: pl.BlockSpec((tile, columns), lambda i: (i, 0))
    outs = [jax.ShapeDtypeStruct((count, c), BF16) for c in (width, hidden, hidden, hidden)]
    return pl.pallas_call(
        expert_kernel,
        grid=(count // tile,),
        out_shape=outs,
        in_specs=[
            by_rows(width),
            pl.BlockSpec(weight_in.shape, lambda i: (0, 0), pipeline_mode=pl.Buffered(1)),
            by_rows(hidden),
        ],
        out_specs=[by_rows(x.shape[1]) for x in outs],
        compiler_params=pltpu.CompilerParams(vmem_limit_bytes=VMEM_LIMIT),
        cost_estimate=cost_of(8 * count * width * hidden, rows, weight_in, grad_act, *outs),
    )(rows, weight_in, grad_act)


def routing_columns(expert_ids, gate_weights):
    high = lax.reduce_precision(gate_weights, 8, 7)
    middle = lax.reduce_precision(gate_weights - high, 8, 7)
    low = gate_weights - high - middle
    columns = jnp.concatenate([expert_ids.astype(F32), high, middle, low], axis=1).astype(BF16)
    return jnp.pad(columns, ((0, 0), (0, 128 - columns.shape[1])))


def route_slots(columns, top):
    planes = lax.axis_size(COLUMN)
    per_plane = lax.axis_size(PLANE) // 2
    tokens = columns.shape[0]
    depth = 3 * tokens * top // (2 * planes * per_plane)
    slots = per_plane * depth
    first = lax.axis_index("zl") * (per_plane * 2) + lax.axis_index("zh") * 2

    def expert_at(place):
        return (first + (place // 2) * 4 + place % 2).astype(F32)

    ids = columns[:, :top].astype(F32)
    experts = expert_at(jnp.arange(per_plane, dtype=jnp.int32))
    named = jnp.any(ids[:, :, None] == experts[None, None, :], axis=1)
    token = jnp.arange(tokens, dtype=jnp.int32)
    before = (token[None, :] < token[:, None]).astype(BF16)
    rank = jnp.dot(before, named.astype(BF16), preferred_element_type=F32)
    rank = jnp.where(named, rank, -1.0).astype(BF16)
    slot = jnp.arange(slots, dtype=jnp.int32)
    place = jnp.arange(per_plane, dtype=jnp.int32)
    spread = (slot[:, None] // depth == place[None, :]).astype(BF16)
    slot_rank = (slot % depth).astype(F32)
    over_tokens = lax.dot_general(
        spread, rank, (((1,), (1,)), ((), ())), preferred_element_type=F32
    )
    chosen = (over_tokens == slot_rank[:, None]).astype(BF16)
    over_slots = lax.dot_general(
        rank, spread, (((1,), (1,)), ((), ())), preferred_element_type=F32
    )
    chosen_back = (over_slots == slot_rank[None, :]).astype(BF16)
    of_slot = jnp.dot(chosen, columns, preferred_element_type=F32)
    gates = (
        of_slot[:, top : 2 * top] + of_slot[:, 2 * top : 3 * top] + of_slot[:, 3 * top : 4 * top]
    )
    mine = of_slot[:, :top] == expert_at(slot // depth)[:, None]
    slot_gate = jnp.sum(jnp.where(mine, gates, 0.0), axis=1, keepdims=True)
    return chosen, chosen_back, slot_gate


def shards(
    hidden_in,
    queries,
    keys,
    values,
    doc_ids,
    norm_gain,
    expert_ids,
    gate_weights,
    w_gate_up,
    w_down,
    grad_out,
):
    row_count = hidden_in.shape[0]
    device_index = lax.axis_index(ALL)
    kv_width = keys.shape[1]

    gathered = []

    def gather_column(part):
        if len(gathered) >= 2:
            part, gathered[-2] = lax.optimization_barrier((part, gathered[-2]))
        rows = lax.all_gather(part, COLUMN, axis=0, tiled=True)
        gathered.append(with_layout_constraint(rows, Layout((0, 1))))

    top = expert_ids.shape[1]
    pieces = columns_of(grad_out, PARTS_GRAD)
    first_width = pieces[0].shape[1]
    pieces[0] = jnp.concatenate([pieces[0], routing_columns(expert_ids, gate_weights)], axis=1)
    for piece in pieces:
        gather_column(piece)

    swap = [(i, i ^ 1) for i in range(lax.axis_size("x"))]
    own_in, own_down = w_gate_up[0], w_down[0]

    doc_columns = jnp.broadcast_to(doc_ids[:, None].astype(BF16), (row_count, 8))
    packed = jnp.concatenate([keys, values, doc_columns], axis=1)
    packed = with_layout_constraint(packed, Layout((1, 0)))
    window_packed = jnp.concatenate(blocks_before(packed) + [packed], axis=0)
    window_packed, own_in, own_down = lax.optimization_barrier((window_packed, own_in, own_down))
    other_down = lax.ppermute(own_down, "x", swap)
    other_in = lax.ppermute(own_in, "x", swap)
    window_keys = window_packed[:, :kv_width]
    window_values = window_packed[:, kv_width : 2 * kv_width]
    window_docs = window_packed[:, 2 * kv_width].astype(jnp.int32)
    query_pos = device_index * row_count + jnp.arange(row_count, dtype=jnp.int32)
    key_pos = (device_index - RIM) * row_count + jnp.arange((RIM + 1) * row_count, dtype=jnp.int32)
    visible = (
        (doc_ids[:, None] == window_docs[None, :])
        & (key_pos[None, :] <= query_pos[:, None])
        & (key_pos[None, :] >= 0)
    )
    attn_out, attn_probs, probs_low = attend_window(queries, window_keys, window_values, visible)
    residual = hidden_in.astype(F32) + attn_out.astype(F32)
    inv_rms = lax.rsqrt(jnp.mean(residual * residual, axis=1, keepdims=True) + EPSILON)
    normed = (residual * inv_rms * norm_gain).astype(BF16)
    normed, other_down = lax.optimization_barrier((normed, other_down))
    for piece in columns_of(normed, PARTS_ROWS):
        if PARTS_GRAD == 1:
            piece, gathered[0] = lax.optimization_barrier((piece, gathered[0]))
        gather_column(piece)
    grad_columns = gathered[:PARTS_GRAD]
    normed_columns = gathered[PARTS_GRAD:]
    chosen, chosen_back, slot_gate = route_slots(grad_columns[0][:, first_width:], top)

    grad_slots = [picked_rows(chosen, part, first_width, slot_gate) for part in grad_columns]
    grad_rows = joined([across_plane(part) for part in grad_slots])
    normed_columns[0], grad_rows, other_in = lax.optimization_barrier(
        (normed_columns[0], grad_rows, other_in)
    )
    weight_in = jnp.concatenate(
        [own_in[:, :HALF], other_in[:, :HALF], own_in[:, HALF:], other_in[:, HALF:]], axis=1
    )
    weight_out = jnp.concatenate([own_down, other_down], axis=0)
    grad_act = lax.dot_general(
        grad_rows, weight_out, (((1,), (1,)), ((), ())), preferred_element_type=F32
    )
    in_rows = joined(
        [across_plane(picked_rows(chosen, part, part.shape[1])) for part in normed_columns]
    )
    back_rows, activated, grad_gate, grad_up = expert_rows(in_rows, weight_in, grad_act)

    chosen_back, _ = lax.optimization_barrier((chosen_back, grad_rows))

    def summed_over_plane(partial):
        return lax.psum_scatter(partial, COLUMN, scatter_dimension=0, tiled=True)

    def added_up(rows):
        return picked_rows(chosen_back, rows, rows.shape[1])

    back_parts = [across_plane(part) for part in columns_of(back_rows, PARTS_BACK)]
    def halves(both, first):
        return both[:, first * HALF : (first + 1) * HALF]

    def times_rows(left, right, out_type):
        return lax.dot_general(
            left, right, (((0,), (0,)), ((), ())), preferred_element_type=F32
        ).astype(out_type)

    own_pre = jnp.concatenate([halves(grad_gate, 0), halves(grad_up, 0)], axis=1)
    other_pre = jnp.concatenate([halves(grad_gate, 1), halves(grad_up, 1)], axis=1)
    sent_in = times_rows(in_rows, other_pre, BF16)
    sent_down = times_rows(halves(activated, 1), grad_rows, BF16)
    kept_in = times_rows(in_rows, own_pre, F32)
    kept_down = times_rows(halves(activated, 0), grad_rows, F32)
    out_rows = [
        jnp.dot(activated, part, preferred_element_type=F32).astype(BF16)
        for part in columns_of(weight_out, PARTS_OUT)
    ]
    back_parts[-1], out_rows[0], sent_in, sent_down, kept_in, kept_down = lax.optimization_barrier(
        (back_parts[-1], out_rows[0], sent_in, sent_down, kept_in, kept_down)
    )
    grad_normed = joined([summed_over_plane(added_up(part)) for part in back_parts]).astype(F32)
    out_parts = [across_plane(part) for part in out_rows]
    sent_in = lax.ppermute(sent_in, "x", swap)
    sent_down = lax.ppermute(sent_down, "x", swap)
    out_sums = [added_up((part.astype(F32) * slot_gate).astype(BF16)) for part in out_parts]
    out_sums[0], sent_in, sent_down = lax.optimization_barrier((out_sums[0], sent_in, sent_down))
    moe_out = joined([summed_over_plane(part) for part in out_sums])

    scaled = norm_gain * grad_normed
    grad_resid = (
        grad_out.astype(F32)
        + inv_rms * scaled
        - residual * inv_rms**3 * jnp.mean(residual * scaled, axis=1, keepdims=True)
    )
    grad_in = grad_resid.astype(BF16)
    grad_queries, key_window_grad, value_window_grad = attend_grad(
        queries, window_keys, window_values, attn_out, grad_in, attn_probs, probs_low
    )
    window_grad = jnp.concatenate([key_window_grad, value_window_grad], axis=1)
    grad_queries, sent_in, sent_down = lax.optimization_barrier((grad_queries, sent_in, sent_down))
    grad_weight_in = kept_in + sent_in.astype(F32)
    grad_weight_out = kept_down + sent_down.astype(F32)
    grad_queries, grad_weight_in, grad_weight_out, moe_out = lax.optimization_barrier(
        (grad_queries, grad_weight_in, grad_weight_out, moe_out)
    )
    output = (residual + moe_out.astype(F32)).astype(BF16)
    far, near = (
        window_grad[i * row_count : (i + 1) * row_count].astype(BF16) for i in range(RIM)
    )
    own_grad = window_grad[RIM * row_count :] + sums_from_after(far, near)
    return (
        output,
        grad_in,
        grad_queries,
        own_grad[:, :kv_width],
        own_grad[:, kv_width:],
        grad_weight_in[None],
        grad_weight_out[None],
    )


def solution(mesh):
    named = Mesh(mesh.devices.reshape(4, 4, 2, 2, 4), ALL)
    rows = P(ALL, None)
    blocks = P(ALL, None, None)
    return jax.shard_map(
        shards,
        mesh=named,
        in_specs=(rows, rows, rows, rows, P(ALL), P(), rows, rows, blocks, blocks, rows),
        out_specs=(rows, rows, rows, rows, rows, blocks, blocks),
        check_vma=False,
    )
```

```python
import jax
import jax.numpy as jnp
from jax import lax
from jax.experimental import pallas as pl
from jax.experimental.layout import Layout, with_layout_constraint
from jax.experimental.pallas import tpu as pltpu
from jax.sharding import Mesh
from jax.sharding import PartitionSpec as P

HEADS = 16
KV_HEADS = 2
HEAD_DIM = 128
GROUP = 8
HALF = 192
RIM = 2

PARTS_GRAD = 1
PARTS_ROWS = 1
PARTS_BACK = 1
PARTS_OUT = 1

VMEM_LIMIT = 60 * 2**20

EPSILON = 1e-06
MASKED = -1e30

ALL = ("zl", "y", "core", "zh", "x")
COLUMN = ("zh", "zl")
PLANE = ("y", "core", "x")

BF16 = jnp.bfloat16
F32 = jnp.float32


def passed_along(block, distance, sources):
    count, line = lax.axis_size(ALL), lax.axis_size("x")
    route = [
        (i, i + distance) for i in range(count) if 0 <= i + distance < count and i % line in sources
    ]
    return lax.ppermute(block, ALL, route)


def blocks_before(block):
    place = lax.axis_index("x")
    near = passed_along(block, 1, (0, 1, 2, 3))
    direct = passed_along(block, 2, (1, 2))
    handed = passed_along(near, 1, (0, 1))
    return [jnp.where((place == 0) | (place == 3), direct, handed), near]


def sums_from_after(far, near):
    place = lax.axis_index("x")
    swap = [(i, i ^ 1) for i in range(lax.axis_size(ALL)) if i % lax.axis_size("x") < 2]
    swapped = lax.ppermute(far, ALL, swap)
    near = jnp.where(place == 0, (near.astype(F32) + swapped.astype(F32)).astype(BF16), near)
    from_near = passed_along(near, -1, (0, 1, 2, 3))
    from_far = passed_along(far, -2, (2, 3))
    from_swapped = passed_along(swapped, -3, (1,))
    return from_near.astype(F32) + jnp.where(place == 2, from_swapped, from_far).astype(F32)


def attend_window(query_rows, window_keys, window_values, visible):
    scale_factor = HEAD_DIM ** (-0.5)
    row_count = query_rows.shape[0]
    query_heads = query_rows.reshape(row_count, KV_HEADS, GROUP, HEAD_DIM)
    key_heads = window_keys.reshape(-1, KV_HEADS, HEAD_DIM)
    value_heads = window_values.reshape(-1, KV_HEADS, HEAD_DIM)
    scores = (
        jnp.einsum("qgmd,kgd->gmqk", query_heads, key_heads, preferred_element_type=F32)
        * scale_factor
    )
    scores = jnp.where(visible[None, None], scores, MASKED)
    row_max = jnp.max(scores, axis=3, keepdims=True)
    exp_terms = jnp.exp(scores - row_max)
    attn_probs = exp_terms / jnp.sum(exp_terms, axis=3, keepdims=True)
    probs_low = attn_probs.astype(BF16)
    mixed_heads = jnp.einsum("gmqk,kgd->qgmd", probs_low, value_heads, preferred_element_type=F32)
    return (
        mixed_heads.reshape(row_count, HEADS * HEAD_DIM).astype(BF16),
        attn_probs,
        probs_low,
    )


def attend_grad(query_rows, window_keys, window_values, attn_out, grad_rows, attn_probs, probs_low):
    scale_factor = HEAD_DIM ** (-0.5)
    row_count = query_rows.shape[0]
    query_heads = query_rows.reshape(row_count, KV_HEADS, GROUP, HEAD_DIM)
    key_heads = window_keys.reshape(-1, KV_HEADS, HEAD_DIM)
    value_heads = window_values.reshape(-1, KV_HEADS, HEAD_DIM)
    grad_heads = grad_rows.reshape(row_count, KV_HEADS, GROUP, HEAD_DIM)
    out_heads = attn_out.reshape(row_count, KV_HEADS, GROUP, HEAD_DIM)
    row_dot = jnp.einsum("qgmd,qgmd->gmq", grad_heads.astype(F32), out_heads.astype(F32))
    grad_probs = jnp.einsum("qgmd,kgd->gmqk", grad_heads, value_heads, preferred_element_type=F32)
    grad_scores = (attn_probs * (grad_probs - row_dot[..., None])).astype(BF16)
    grad_query = (
        jnp.einsum("gmqk,kgd->qgmd", grad_scores, key_heads, preferred_element_type=F32)
        * scale_factor
    )
    grad_key = (
        jnp.einsum("gmqk,qgmd->kgd", grad_scores, query_heads, preferred_element_type=F32)
        * scale_factor
    )
    grad_value = jnp.einsum("gmqk,qgmd->kgd", probs_low, grad_heads, preferred_element_type=F32)
    return (
        grad_query.reshape(row_count, HEADS * HEAD_DIM).astype(BF16),
        grad_key.reshape(-1, KV_HEADS * HEAD_DIM),
        grad_value.reshape(-1, KV_HEADS * HEAD_DIM),
    )


def columns_of(array, parts):
    width = array.shape[1] // parts
    return [array[:, i * width : (i + 1) * width] for i in range(parts)]


def joined(parts):
    return parts[0] if len(parts) == 1 else jnp.concatenate(parts, axis=1)


def across_plane(rows):
    pairs, line = lax.axis_size(PLANE) // lax.axis_size("x"), lax.axis_size("x")
    groups = [[i * line + x for i in range(pairs) for x in places] for places in ((0, 3), (1, 2))]
    count = len(groups[0])
    cut = rows.reshape(count, rows.shape[0] // count, rows.shape[1])
    moved = lax.all_to_all(cut, PLANE, 0, 0, axis_index_groups=groups, tiled=True)
    return moved.reshape(rows.shape)


def cost_of(flops, *arrays):
    return pl.CostEstimate(
        flops=flops,
        bytes_accessed=sum(x.size * x.dtype.itemsize for x in arrays),
        transcendentals=0,
    )


def pick_kernel(chosen_ref, rows_ref, *rest):
    out_ref = rest[-1]
    picked = jnp.dot(chosen_ref[...], rows_ref[...], preferred_element_type=F32)
    if len(rest) == 2:
        picked = picked * rest[0][...]
    out_ref[...] = picked.astype(out_ref.dtype)


def picked_rows(chosen, rows, width, scale=None):
    count, depth = chosen.shape
    tile = 512
    out = jax.ShapeDtypeStruct((count, width), BF16)
    whole = pl.BlockSpec((count, depth), lambda i: (0, 0), pipeline_mode=pl.Buffered(1))
    operands = [chosen, rows]
    specs = [whole, pl.BlockSpec((depth, tile), lambda i: (0, i))]
    if scale is not None:
        operands.append(scale)
        specs.append(pl.BlockSpec((count, 1), lambda i: (0, 0)))
    return pl.pallas_call(
        pick_kernel,
        grid=(width // tile,),
        out_shape=out,
        in_specs=specs,
        out_specs=pl.BlockSpec((count, tile), lambda i: (0, i)),
        compiler_params=pltpu.CompilerParams(vmem_limit_bytes=VMEM_LIMIT),
        cost_estimate=cost_of(2 * count * depth * width, chosen, rows, out),
    )(*operands)


def expert_kernel(rows_ref, weight_ref, grad_act_ref, half_ref, act_ref, gate_ref, up_ref):
    projected = jnp.dot(rows_ref[...], weight_ref[...], preferred_element_type=F32)
    gate_pre = projected[:, : 2 * HALF]
    up_pre = projected[:, 2 * HALF :]
    sigmoid_gate = jax.nn.sigmoid(gate_pre)
    silu = gate_pre * sigmoid_gate
    act_ref[...] = (silu * up_pre).astype(BF16)
    grad_act = grad_act_ref[...]
    grad_gate = (grad_act * up_pre * sigmoid_gate * (1.0 + gate_pre * (1.0 - sigmoid_gate))).astype(
        BF16
    )
    grad_up = (grad_act * silu).astype(BF16)
    gate_ref[...] = grad_gate
    up_ref[...] = grad_up
    half_ref[...] = lax.dot_general(
        jnp.concatenate([grad_gate, grad_up], axis=1),
        weight_ref[...],
        (((1,), (1,)), ((), ())),
        preferred_element_type=F32,
    ).astype(BF16)


def expert_rows(rows, weight_in, grad_act):
    count, width = rows.shape
    hidden = grad_act.shape[1]
    tile = 256
    by_rows = lambda columns: pl.BlockSpec((tile, columns), lambda i: (i, 0))
    outs = [jax.ShapeDtypeStruct((count, c), BF16) for c in (width, hidden, hidden, hidden)]
    return pl.pallas_call(
        expert_kernel,
        grid=(count // tile,),
        out_shape=outs,
        in_specs=[
            by_rows(width),
            pl.BlockSpec(weight_in.shape, lambda i: (0, 0), pipeline_mode=pl.Buffered(1)),
            by_rows(hidden),
        ],
        out_specs=[by_rows(x.shape[1]) for x in outs],
        compiler_params=pltpu.CompilerParams(vmem_limit_bytes=VMEM_LIMIT),
        cost_estimate=cost_of(8 * count * width * hidden, rows, weight_in, grad_act, *outs),
    )(rows, weight_in, grad_act)


def routing_columns(expert_ids, gate_weights):
    high = lax.reduce_precision(gate_weights, 8, 7)
    middle = lax.reduce_precision(gate_weights - high, 8, 7)
    low = gate_weights - high - middle
    columns = jnp.concatenate([expert_ids.astype(F32), high, middle, low], axis=1).astype(BF16)
    return jnp.pad(columns, ((0, 0), (0, 128 - columns.shape[1])))


def route_slots(columns, top):
    planes = lax.axis_size(COLUMN)
    per_plane = lax.axis_size(PLANE) // 2
    tokens = columns.shape[0]
    depth = 3 * tokens * top // (2 * planes * per_plane)
    slots = per_plane * depth
    first = lax.axis_index("zl") * (per_plane * 2) + lax.axis_index("zh") * 2

    def expert_at(place):
        return (first + (place // 2) * 4 + place % 2).astype(F32)

    ids = columns[:, :top].astype(F32)
    experts = expert_at(jnp.arange(per_plane, dtype=jnp.int32))
    named = jnp.any(ids[:, :, None] == experts[None, None, :], axis=1)
    token = jnp.arange(tokens, dtype=jnp.int32)
    before = (token[None, :] < token[:, None]).astype(BF16)
    rank = jnp.dot(before, named.astype(BF16), preferred_element_type=F32)
    rank = jnp.where(named, rank, -1.0).astype(BF16)
    slot = jnp.arange(slots, dtype=jnp.int32)
    place = jnp.arange(per_plane, dtype=jnp.int32)
    spread = (slot[:, None] // depth == place[None, :]).astype(BF16)
    slot_rank = (slot % depth).astype(F32)
    over_tokens = lax.dot_general(
        spread, rank, (((1,), (1,)), ((), ())), preferred_element_type=F32
    )
    chosen = (over_tokens == slot_rank[:, None]).astype(BF16)
    over_slots = lax.dot_general(
        rank, spread, (((1,), (1,)), ((), ())), preferred_element_type=F32
    )
    chosen_back = (over_slots == slot_rank[None, :]).astype(BF16)
    of_slot = jnp.dot(chosen, columns, preferred_element_type=F32)
    gates = (
        of_slot[:, top : 2 * top] + of_slot[:, 2 * top : 3 * top] + of_slot[:, 3 * top : 4 * top]
    )
    mine = of_slot[:, :top] == expert_at(slot // depth)[:, None]
    slot_gate = jnp.sum(jnp.where(mine, gates, 0.0), axis=1, keepdims=True)
    gated_back = chosen_back * slot_gate.reshape(1, -1).astype(BF16)
    return chosen, chosen_back, gated_back, slot_gate


def shards(
    hidden_in,
    queries,
    keys,
    values,
    doc_ids,
    norm_gain,
    expert_ids,
    gate_weights,
    w_gate_up,
    w_down,
    grad_out,
):
    row_count = hidden_in.shape[0]
    device_index = lax.axis_index(ALL)
    kv_width = keys.shape[1]

    gathered = []

    def gather_column(part):
        if len(gathered) >= 2:
            part, gathered[-2] = lax.optimization_barrier((part, gathered[-2]))
        rows = lax.all_gather(part, COLUMN, axis=0, tiled=True)
        gathered.append(with_layout_constraint(rows, Layout((0, 1))))

    top = expert_ids.shape[1]
    pieces = columns_of(grad_out, PARTS_GRAD)
    first_width = pieces[0].shape[1]
    pieces[0] = jnp.concatenate([pieces[0], routing_columns(expert_ids, gate_weights)], axis=1)
    for piece in pieces:
        gather_column(piece)

    swap = [(i, i ^ 1) for i in range(lax.axis_size("x"))]
    own_in, own_down = w_gate_up[0], w_down[0]

    doc_columns = jnp.broadcast_to(doc_ids[:, None].astype(BF16), (row_count, 8))
    packed = jnp.concatenate([keys, values, doc_columns], axis=1)
    packed = with_layout_constraint(packed, Layout((1, 0)))
    window_packed = jnp.concatenate(blocks_before(packed) + [packed], axis=0)
    window_packed, own_in, own_down = lax.optimization_barrier((window_packed, own_in, own_down))
    other_down = lax.ppermute(own_down, "x", swap)
    other_in = lax.ppermute(own_in, "x", swap)
    window_keys = window_packed[:, :kv_width]
    window_values = window_packed[:, kv_width : 2 * kv_width]
    window_docs = window_packed[:, 2 * kv_width].astype(jnp.int32)
    query_pos = device_index * row_count + jnp.arange(row_count, dtype=jnp.int32)
    key_pos = (device_index - RIM) * row_count + jnp.arange((RIM + 1) * row_count, dtype=jnp.int32)
    visible = (
        (doc_ids[:, None] == window_docs[None, :])
        & (key_pos[None, :] <= query_pos[:, None])
        & (key_pos[None, :] >= 0)
    )
    attn_out, attn_probs, probs_low = attend_window(queries, window_keys, window_values, visible)
    residual = hidden_in.astype(F32) + attn_out.astype(F32)
    inv_rms = lax.rsqrt(jnp.mean(residual * residual, axis=1, keepdims=True) + EPSILON)
    normed = (residual * inv_rms * norm_gain).astype(BF16)
    normed, other_down = lax.optimization_barrier((normed, other_down))
    for piece in columns_of(normed, PARTS_ROWS):
        if PARTS_GRAD == 1:
            piece, gathered[0] = lax.optimization_barrier((piece, gathered[0]))
        gather_column(piece)
    grad_columns = gathered[:PARTS_GRAD]
    normed_columns = gathered[PARTS_GRAD:]
    chosen, chosen_back, gated_back, slot_gate = route_slots(grad_columns[0][:, first_width:], top)

    grad_slots = [picked_rows(chosen, part, first_width, slot_gate) for part in grad_columns]
    grad_rows = joined([across_plane(part) for part in grad_slots])
    normed_columns[0], grad_rows, other_in = lax.optimization_barrier(
        (normed_columns[0], grad_rows, other_in)
    )
    weight_in = jnp.concatenate(
        [own_in[:, :HALF], other_in[:, :HALF], own_in[:, HALF:], other_in[:, HALF:]], axis=1
    )
    weight_out = jnp.concatenate([own_down, other_down], axis=0)
    grad_act = lax.dot_general(
        grad_rows, weight_out, (((1,), (1,)), ((), ())), preferred_element_type=F32
    )
    in_rows = joined(
        [across_plane(picked_rows(chosen, part, part.shape[1])) for part in normed_columns]
    )
    back_rows, activated, grad_gate, grad_up = expert_rows(in_rows, weight_in, grad_act)

    chosen_back, gated_back, _ = lax.optimization_barrier((chosen_back, gated_back, grad_rows))

    def summed_over_plane(partial):
        return lax.psum_scatter(partial, COLUMN, scatter_dimension=0, tiled=True)

    def added_up(weights, rows):
        return picked_rows(weights, rows, rows.shape[1])

    back_parts = [across_plane(part) for part in columns_of(back_rows, PARTS_BACK)]
    def halves(both, first):
        return both[:, first * HALF : (first + 1) * HALF]

    def times_rows(left, right, out_type):
        return lax.dot_general(
            left, right, (((0,), (0,)), ((), ())), preferred_element_type=F32
        ).astype(out_type)

    own_pre = jnp.concatenate([halves(grad_gate, 0), halves(grad_up, 0)], axis=1)
    other_pre = jnp.concatenate([halves(grad_gate, 1), halves(grad_up, 1)], axis=1)
    sent_in = times_rows(in_rows, other_pre, BF16)
    sent_down = times_rows(halves(activated, 1), grad_rows, BF16)
    kept_in = times_rows(in_rows, own_pre, F32)
    kept_down = times_rows(halves(activated, 0), grad_rows, F32)
    out_rows = [
        jnp.dot(activated, part, preferred_element_type=F32).astype(BF16)
        for part in columns_of(weight_out, PARTS_OUT)
    ]
    back_parts[-1], out_rows[0], sent_in, sent_down, kept_in, kept_down = lax.optimization_barrier(
        (back_parts[-1], out_rows[0], sent_in, sent_down, kept_in, kept_down)
    )
    grad_normed = joined([summed_over_plane(added_up(chosen_back, part)) for part in back_parts])
    out_parts = [across_plane(part) for part in out_rows]
    sent_in = lax.ppermute(sent_in, "x", swap)
    out_parts[-1], sent_down = lax.optimization_barrier((out_parts[-1], sent_down))
    sent_down = lax.ppermute(sent_down, "x", swap)
    out_sums = [added_up(gated_back, part) for part in out_parts]
    out_sums[0], sent_in = lax.optimization_barrier((out_sums[0], sent_in))
    moe_out = joined([summed_over_plane(part) for part in out_sums])

    scaled = norm_gain * grad_normed.astype(F32)
    grad_resid = (
        grad_out.astype(F32)
        + inv_rms * scaled
        - residual * inv_rms**3 * jnp.mean(residual * scaled, axis=1, keepdims=True)
    )
    grad_in = grad_resid.astype(BF16)
    grad_queries, key_window_grad, value_window_grad = attend_grad(
        queries, window_keys, window_values, attn_out, grad_in, attn_probs, probs_low
    )
    window_grad = jnp.concatenate([key_window_grad, value_window_grad], axis=1)
    grad_queries, sent_in, sent_down = lax.optimization_barrier((grad_queries, sent_in, sent_down))
    grad_weight_in = kept_in + sent_in.astype(F32)
    grad_weight_out = kept_down + sent_down.astype(F32)
    grad_queries, grad_weight_in, grad_weight_out, moe_out = lax.optimization_barrier(
        (grad_queries, grad_weight_in, grad_weight_out, moe_out)
    )
    output = (residual + moe_out.astype(F32)).astype(BF16)
    far, near = (
        window_grad[i * row_count : (i + 1) * row_count].astype(BF16) for i in range(RIM)
    )
    own_grad = window_grad[RIM * row_count :] + sums_from_after(far, near)
    return (
        output,
        grad_in,
        grad_queries,
        own_grad[:, :kv_width],
        own_grad[:, kv_width:],
        grad_weight_in[None],
        grad_weight_out[None],
    )


def solution(mesh):
    named = Mesh(mesh.devices.reshape(4, 4, 2, 2, 4), ALL)
    rows = P(ALL, None)
    blocks = P(ALL, None, None)
    return jax.shard_map(
        shards,
        mesh=named,
        in_specs=(rows, rows, rows, rows, P(ALL), P(), rows, rows, blocks, blocks, rows),
        out_specs=(rows, rows, rows, rows, rows, blocks, blocks),
        check_vma=False,
    )
```

```python
import jax
import jax.numpy as jnp
from jax import lax
from jax.experimental import pallas as pl
from jax.experimental.layout import Layout, with_layout_constraint
from jax.experimental.pallas import tpu as pltpu
from jax.sharding import Mesh
from jax.sharding import PartitionSpec as P

HEADS = 16
KV_HEADS = 2
HEAD_DIM = 128
GROUP = 8
HALF = 192
RIM = 2

PARTS_GRAD = 1
PARTS_ROWS = 1
PARTS_BACK = 1
PARTS_OUT = 1

VMEM_LIMIT = 60 * 2**20

EPSILON = 1e-06
MASKED = -1e30

ALL = ("zl", "y", "core", "zh", "x")
COLUMN = ("zh", "zl")
PLANE = ("y", "core", "x")

BF16 = jnp.bfloat16
F32 = jnp.float32


def passed_along(block, distance, sources):
    count, line = lax.axis_size(ALL), lax.axis_size("x")
    route = [
        (i, i + distance) for i in range(count) if 0 <= i + distance < count and i % line in sources
    ]
    return lax.ppermute(block, ALL, route)


def blocks_before(block):
    place = lax.axis_index("x")
    near = passed_along(block, 1, (0, 1, 2, 3))
    direct = passed_along(block, 2, (1, 2))
    handed = passed_along(near, 1, (0, 1))
    return [jnp.where((place == 0) | (place == 3), direct, handed), near]


def sums_from_after(far, near):
    place = lax.axis_index("x")
    swap = [(i, i ^ 1) for i in range(lax.axis_size(ALL)) if i % lax.axis_size("x") < 2]
    swapped = lax.ppermute(far, ALL, swap)
    near = jnp.where(place == 0, (near.astype(F32) + swapped.astype(F32)).astype(BF16), near)
    from_near = passed_along(near, -1, (0, 1, 2, 3))
    from_far = passed_along(far, -2, (2, 3))
    from_swapped = passed_along(swapped, -3, (1,))
    return from_near.astype(F32) + jnp.where(place == 2, from_swapped, from_far).astype(F32)


def attend_window(query_rows, window_keys, window_values, visible):
    scale_factor = HEAD_DIM ** (-0.5)
    row_count = query_rows.shape[0]
    query_heads = query_rows.reshape(row_count, KV_HEADS, GROUP, HEAD_DIM)
    key_heads = window_keys.reshape(-1, KV_HEADS, HEAD_DIM)
    value_heads = window_values.reshape(-1, KV_HEADS, HEAD_DIM)
    scores = (
        jnp.einsum("qgmd,kgd->gmqk", query_heads, key_heads, preferred_element_type=F32)
        * scale_factor
    )
    scores = jnp.where(visible[None, None], scores, MASKED)
    row_max = jnp.max(scores, axis=3, keepdims=True)
    exp_terms = jnp.exp(scores - row_max)
    attn_probs = exp_terms / jnp.sum(exp_terms, axis=3, keepdims=True)
    probs_low = attn_probs.astype(BF16)
    mixed_heads = jnp.einsum("gmqk,kgd->qgmd", probs_low, value_heads, preferred_element_type=F32)
    return (
        mixed_heads.reshape(row_count, HEADS * HEAD_DIM).astype(BF16),
        attn_probs,
        probs_low,
    )


def attend_grad(query_rows, window_keys, window_values, attn_out, grad_rows, attn_probs, probs_low):
    scale_factor = HEAD_DIM ** (-0.5)
    row_count = query_rows.shape[0]
    query_heads = query_rows.reshape(row_count, KV_HEADS, GROUP, HEAD_DIM)
    key_heads = window_keys.reshape(-1, KV_HEADS, HEAD_DIM)
    value_heads = window_values.reshape(-1, KV_HEADS, HEAD_DIM)
    grad_heads = grad_rows.reshape(row_count, KV_HEADS, GROUP, HEAD_DIM)
    out_heads = attn_out.reshape(row_count, KV_HEADS, GROUP, HEAD_DIM)
    row_dot = jnp.einsum("qgmd,qgmd->gmq", grad_heads.astype(F32), out_heads.astype(F32))
    grad_probs = jnp.einsum("qgmd,kgd->gmqk", grad_heads, value_heads, preferred_element_type=F32)
    grad_scores = (attn_probs * (grad_probs - row_dot[..., None])).astype(BF16)
    grad_query = (
        jnp.einsum("gmqk,kgd->qgmd", grad_scores, key_heads, preferred_element_type=F32)
        * scale_factor
    )
    grad_key = (
        jnp.einsum("gmqk,qgmd->kgd", grad_scores, query_heads, preferred_element_type=F32)
        * scale_factor
    )
    grad_value = jnp.einsum("gmqk,qgmd->kgd", probs_low, grad_heads, preferred_element_type=F32)
    return (
        grad_query.reshape(row_count, HEADS * HEAD_DIM).astype(BF16),
        grad_key.reshape(-1, KV_HEADS * HEAD_DIM),
        grad_value.reshape(-1, KV_HEADS * HEAD_DIM),
    )


def columns_of(array, parts):
    width = array.shape[1] // parts
    return [array[:, i * width : (i + 1) * width] for i in range(parts)]


def joined(parts):
    return parts[0] if len(parts) == 1 else jnp.concatenate(parts, axis=1)


def across_plane(rows):
    pairs, line = lax.axis_size(PLANE) // lax.axis_size("x"), lax.axis_size("x")
    groups = [[i * line + x for i in range(pairs) for x in places] for places in ((0, 3), (1, 2))]
    count = len(groups[0])
    cut = rows.reshape(count, rows.shape[0] // count, rows.shape[1])
    moved = lax.all_to_all(cut, PLANE, 0, 0, axis_index_groups=groups, tiled=True)
    return moved.reshape(rows.shape)


def cost_of(flops, *arrays):
    return pl.CostEstimate(
        flops=flops,
        bytes_accessed=sum(x.size * x.dtype.itemsize for x in arrays),
        transcendentals=0,
    )


def pick_kernel(chosen_ref, rows_ref, *rest):
    out_ref = rest[-1]
    picked = jnp.dot(chosen_ref[...], rows_ref[...], preferred_element_type=F32)
    if len(rest) == 2:
        picked = picked * rest[0][...]
    out_ref[...] = picked.astype(out_ref.dtype)


def picked_rows(chosen, rows, width, scale=None):
    count, depth = chosen.shape
    tile = count // 2
    out = jax.ShapeDtypeStruct((count, width), BF16)
    whole = pl.BlockSpec((depth, width), lambda i: (0, 0), pipeline_mode=pl.Buffered(1))
    operands = [chosen, rows]
    specs = [pl.BlockSpec((tile, depth), lambda i: (i, 0)), whole]
    if scale is not None:
        operands.append(scale)
        specs.append(pl.BlockSpec((tile, 1), lambda i: (i, 0)))
    return pl.pallas_call(
        pick_kernel,
        grid=(count // tile,),
        out_shape=out,
        in_specs=specs,
        out_specs=pl.BlockSpec((tile, width), lambda i: (i, 0)),
        compiler_params=pltpu.CompilerParams(vmem_limit_bytes=VMEM_LIMIT),
        cost_estimate=cost_of(2 * count * depth * width, chosen, rows, out),
    )(*operands)


def expert_kernel(rows_ref, weight_ref, grad_act_ref, half_ref, act_ref, gate_ref, up_ref):
    projected = jnp.dot(rows_ref[...], weight_ref[...], preferred_element_type=F32)
    gate_pre = projected[:, : 2 * HALF]
    up_pre = projected[:, 2 * HALF :]
    sigmoid_gate = jax.nn.sigmoid(gate_pre)
    silu = gate_pre * sigmoid_gate
    act_ref[...] = (silu * up_pre).astype(BF16)
    grad_act = grad_act_ref[...]
    grad_gate = (grad_act * up_pre * sigmoid_gate * (1.0 + gate_pre * (1.0 - sigmoid_gate))).astype(
        BF16
    )
    grad_up = (grad_act * silu).astype(BF16)
    gate_ref[...] = grad_gate
    up_ref[...] = grad_up
    half_ref[...] = lax.dot_general(
        jnp.concatenate([grad_gate, grad_up], axis=1),
        weight_ref[...],
        (((1,), (1,)), ((), ())),
        preferred_element_type=F32,
    ).astype(BF16)


def expert_rows(rows, weight_in, grad_act):
    count, width = rows.shape
    hidden = grad_act.shape[1]
    tile = 256
    by_rows = lambda columns: pl.BlockSpec((tile, columns), lambda i: (i, 0))
    outs = [jax.ShapeDtypeStruct((count, c), BF16) for c in (width, hidden, hidden, hidden)]
    return pl.pallas_call(
        expert_kernel,
        grid=(count // tile,),
        out_shape=outs,
        in_specs=[
            by_rows(width),
            pl.BlockSpec(weight_in.shape, lambda i: (0, 0), pipeline_mode=pl.Buffered(1)),
            by_rows(hidden),
        ],
        out_specs=[by_rows(x.shape[1]) for x in outs],
        compiler_params=pltpu.CompilerParams(vmem_limit_bytes=VMEM_LIMIT),
        cost_estimate=cost_of(8 * count * width * hidden, rows, weight_in, grad_act, *outs),
    )(rows, weight_in, grad_act)


def routing_columns(expert_ids, gate_weights):
    high = lax.reduce_precision(gate_weights, 8, 7)
    middle = lax.reduce_precision(gate_weights - high, 8, 7)
    low = gate_weights - high - middle
    columns = jnp.concatenate([expert_ids.astype(F32), high, middle, low], axis=1).astype(BF16)
    return jnp.pad(columns, ((0, 0), (0, 128 - columns.shape[1])))


def route_slots(columns, top):
    planes = lax.axis_size(COLUMN)
    per_plane = lax.axis_size(PLANE) // 2
    tokens = columns.shape[0]
    depth = 3 * tokens * top // (2 * planes * per_plane)
    slots = per_plane * depth
    first = lax.axis_index("zl") * (per_plane * 2) + lax.axis_index("zh") * 2

    def expert_at(place):
        return (first + (place // 2) * 4 + place % 2).astype(F32)

    ids = columns[:, :top].astype(F32)
    experts = expert_at(jnp.arange(per_plane, dtype=jnp.int32))
    named = jnp.any(ids[:, :, None] == experts[None, None, :], axis=1)
    token = jnp.arange(tokens, dtype=jnp.int32)
    before = (token[None, :] < token[:, None]).astype(BF16)
    rank = jnp.dot(before, named.astype(BF16), preferred_element_type=F32)
    rank = jnp.where(named, rank, -1.0).astype(BF16)
    slot = jnp.arange(slots, dtype=jnp.int32)
    place = jnp.arange(per_plane, dtype=jnp.int32)
    spread = (slot[:, None] // depth == place[None, :]).astype(BF16)
    slot_rank = (slot % depth).astype(F32)
    over_tokens = lax.dot_general(
        spread, rank, (((1,), (1,)), ((), ())), preferred_element_type=F32
    )
    chosen = (over_tokens == slot_rank[:, None]).astype(BF16)
    over_slots = lax.dot_general(
        rank, spread, (((1,), (1,)), ((), ())), preferred_element_type=F32
    )
    chosen_back = (over_slots == slot_rank[None, :]).astype(BF16)
    of_slot = jnp.dot(chosen, columns, preferred_element_type=F32)
    gates = (
        of_slot[:, top : 2 * top] + of_slot[:, 2 * top : 3 * top] + of_slot[:, 3 * top : 4 * top]
    )
    mine = of_slot[:, :top] == expert_at(slot // depth)[:, None]
    slot_gate = jnp.sum(jnp.where(mine, gates, 0.0), axis=1, keepdims=True)
    gated_back = chosen_back * slot_gate.reshape(1, -1).astype(BF16)
    return chosen, chosen_back, gated_back, slot_gate


def shards(
    hidden_in,
    queries,
    keys,
    values,
    doc_ids,
    norm_gain,
    expert_ids,
    gate_weights,
    w_gate_up,
    w_down,
    grad_out,
):
    row_count = hidden_in.shape[0]
    device_index = lax.axis_index(ALL)
    kv_width = keys.shape[1]

    gathered = []

    def gather_column(part):
        if len(gathered) >= 2:
            part, gathered[-2] = lax.optimization_barrier((part, gathered[-2]))
        rows = lax.all_gather(part, COLUMN, axis=0, tiled=True)
        gathered.append(with_layout_constraint(rows, Layout((0, 1))))

    top = expert_ids.shape[1]
    pieces = columns_of(grad_out, PARTS_GRAD)
    first_width = pieces[0].shape[1]
    pieces[0] = jnp.concatenate([pieces[0], routing_columns(expert_ids, gate_weights)], axis=1)
    for piece in pieces:
        gather_column(piece)

    swap = [(i, i ^ 1) for i in range(lax.axis_size("x"))]
    own_in, own_down = w_gate_up[0], w_down[0]

    doc_columns = jnp.broadcast_to(doc_ids[:, None].astype(BF16), (row_count, 8))
    packed = jnp.concatenate([keys, values, doc_columns], axis=1)
    packed = with_layout_constraint(packed, Layout((1, 0)))
    window_packed = jnp.concatenate(blocks_before(packed) + [packed], axis=0)
    window_packed, own_in, own_down = lax.optimization_barrier((window_packed, own_in, own_down))
    other_down = lax.ppermute(own_down, "x", swap)
    other_in = lax.ppermute(own_in, "x", swap)
    window_keys = window_packed[:, :kv_width]
    window_values = window_packed[:, kv_width : 2 * kv_width]
    window_docs = window_packed[:, 2 * kv_width].astype(jnp.int32)
    query_pos = device_index * row_count + jnp.arange(row_count, dtype=jnp.int32)
    key_pos = (device_index - RIM) * row_count + jnp.arange((RIM + 1) * row_count, dtype=jnp.int32)
    visible = (
        (doc_ids[:, None] == window_docs[None, :])
        & (key_pos[None, :] <= query_pos[:, None])
        & (key_pos[None, :] >= 0)
    )
    attn_out, attn_probs, probs_low = attend_window(queries, window_keys, window_values, visible)
    residual = hidden_in.astype(F32) + attn_out.astype(F32)
    inv_rms = lax.rsqrt(jnp.mean(residual * residual, axis=1, keepdims=True) + EPSILON)
    normed = (residual * inv_rms * norm_gain).astype(BF16)
    normed, other_down = lax.optimization_barrier((normed, other_down))
    for piece in columns_of(normed, PARTS_ROWS):
        if PARTS_GRAD == 1:
            piece, gathered[0] = lax.optimization_barrier((piece, gathered[0]))
        gather_column(piece)
    grad_columns = gathered[:PARTS_GRAD]
    normed_columns = gathered[PARTS_GRAD:]
    chosen, chosen_back, gated_back, slot_gate = route_slots(grad_columns[0][:, first_width:], top)

    grad_slots = [picked_rows(chosen, part, first_width, slot_gate) for part in grad_columns]
    grad_rows = joined([across_plane(part) for part in grad_slots])
    normed_columns[0], grad_rows, other_in = lax.optimization_barrier(
        (normed_columns[0], grad_rows, other_in)
    )
    weight_in = jnp.concatenate(
        [own_in[:, :HALF], other_in[:, :HALF], own_in[:, HALF:], other_in[:, HALF:]], axis=1
    )
    weight_out = jnp.concatenate([own_down, other_down], axis=0)
    grad_act = lax.dot_general(
        grad_rows, weight_out, (((1,), (1,)), ((), ())), preferred_element_type=F32
    )
    in_rows = joined(
        [across_plane(picked_rows(chosen, part, part.shape[1])) for part in normed_columns]
    )
    back_rows, activated, grad_gate, grad_up = expert_rows(in_rows, weight_in, grad_act)

    chosen_back, gated_back, _ = lax.optimization_barrier((chosen_back, gated_back, grad_rows))

    def summed_over_plane(partial):
        return lax.psum_scatter(partial, COLUMN, scatter_dimension=0, tiled=True)

    def added_up(weights, rows):
        return picked_rows(weights, rows, rows.shape[1])

    back_parts = [across_plane(part) for part in columns_of(back_rows, PARTS_BACK)]
    def halves(both, first):
        return both[:, first * HALF : (first + 1) * HALF]

    def times_rows(left, right, out_type):
        return lax.dot_general(
            left, right, (((0,), (0,)), ((), ())), preferred_element_type=F32
        ).astype(out_type)

    own_pre = jnp.concatenate([halves(grad_gate, 0), halves(grad_up, 0)], axis=1)
    other_pre = jnp.concatenate([halves(grad_gate, 1), halves(grad_up, 1)], axis=1)
    sent_in = times_rows(in_rows, other_pre, BF16)
    sent_down = times_rows(halves(activated, 1), grad_rows, BF16)
    kept_in = times_rows(in_rows, own_pre, F32)
    kept_down = times_rows(halves(activated, 0), grad_rows, F32)
    out_rows = [
        jnp.dot(activated, part, preferred_element_type=F32).astype(BF16)
        for part in columns_of(weight_out, PARTS_OUT)
    ]
    back_parts[-1], out_rows[0], sent_in, sent_down, kept_in, kept_down = lax.optimization_barrier(
        (back_parts[-1], out_rows[0], sent_in, sent_down, kept_in, kept_down)
    )
    grad_normed = joined([summed_over_plane(added_up(chosen_back, part)) for part in back_parts])
    out_parts = [across_plane(part) for part in out_rows]
    sent_in = lax.ppermute(sent_in, "x", swap)
    out_parts[-1], sent_down = lax.optimization_barrier((out_parts[-1], sent_down))
    sent_down = lax.ppermute(sent_down, "x", swap)
    out_sums = [added_up(gated_back, part) for part in out_parts]
    out_sums[0], sent_in = lax.optimization_barrier((out_sums[0], sent_in))
    moe_out = joined([summed_over_plane(part) for part in out_sums])

    scaled = norm_gain * grad_normed.astype(F32)
    grad_resid = (
        grad_out.astype(F32)
        + inv_rms * scaled
        - residual * inv_rms**3 * jnp.mean(residual * scaled, axis=1, keepdims=True)
    )
    grad_in = grad_resid.astype(BF16)
    grad_queries, key_window_grad, value_window_grad = attend_grad(
        queries, window_keys, window_values, attn_out, grad_in, attn_probs, probs_low
    )
    window_grad = jnp.concatenate([key_window_grad, value_window_grad], axis=1)
    grad_queries, sent_in, sent_down = lax.optimization_barrier((grad_queries, sent_in, sent_down))
    grad_weight_in = kept_in + sent_in.astype(F32)
    grad_weight_out = kept_down + sent_down.astype(F32)
    grad_weight_in, grad_weight_out, moe_out = lax.optimization_barrier(
        (grad_weight_in, grad_weight_out, moe_out)
    )
    output = (residual + moe_out.astype(F32)).astype(BF16)
    far, near = (
        window_grad[i * row_count : (i + 1) * row_count].astype(BF16) for i in range(RIM)
    )
    own_grad = window_grad[RIM * row_count :] + sums_from_after(far, near)
    return (
        output,
        grad_in,
        grad_queries,
        own_grad[:, :kv_width],
        own_grad[:, kv_width:],
        grad_weight_in[None],
        grad_weight_out[None],
    )


def solution(mesh):
    named = Mesh(mesh.devices.reshape(4, 4, 2, 2, 4), ALL)
    rows = P(ALL, None)
    blocks = P(ALL, None, None)
    return jax.shard_map(
        shards,
        mesh=named,
        in_specs=(rows, rows, rows, rows, P(ALL), P(), rows, rows, blocks, blocks, rows),
        out_specs=(rows, rows, rows, rows, rows, blocks, blocks),
        check_vma=False,
    )
```
